32 devices in a mesh: band: 8 (over z, core), grid: 4 (over y, x).
Axes of the slice: x: 2, y: 2, z: 4, core: 2. Of those that a mesh axis runs over, the one named last changes fastest.
Arguments:
- orbitals: float32 [8, 128, 128, 128], P('band', 'grid'), may hold values from -6 to 6
Outputs:
- exchange_field: float32 [8, 128, 128, 128], P('band', 'grid')
The draws below stay inside these ranges and needn't reach their ends.
All inputs are finite; a program needn't handle non-finite values.
Results may differ from the reference program's by a relative error of at most 0.0001.
Values sent between devices are 32-bit elements; how exact they have to be, the bound alone decides.
A program may use at most 128 MiB of HBM per device.

```python
import jax
import jax.numpy as jnp
from jax import lax

NX = 128
NY = 128
NZ = 128
ORB_DEV = 1
ORBITALS = 8


def shard_levels(stream_key, extent, shards, low, high):
    def one(axis_at, blocks):
        draws = jax.random.uniform(jax.random.fold_in(jax.random.fold_in(stream_key, 6), axis_at), (blocks,), jnp.float32, low / len(shards), high / len(shards))
        return jnp.repeat(jnp.exp(draws), extent[axis_at] // blocks).reshape((-1,) + (1,) * (len(extent) - axis_at - 1))

    factor_of = one(*shards[0])
    for cut in shards[1:]:
        factor_of = factor_of * one(*cut)
    return factor_of


def gaussian(stream_key, extent, width, bound, split=(), held_as=jnp.bfloat16):
    drawn = width * jax.random.normal(stream_key, extent, jnp.float32)
    if split:
        drawn = drawn * shard_levels(stream_key, extent, split, -0.22, 0.18)
    return jnp.clip(drawn, -bound, bound).astype(held_as)


def setup_inputs(seed: int = 0) -> dict:
    keys = jax.random.split(jax.random.key(seed), 2)
    orbitals = gaussian(keys[0], (ORBITALS, NX, NY, NZ), 1.0, 6.0, ((0, 8), (1, 4)), jnp.float32)
    return {"orbitals": orbitals}


coulomb_scale = 64.0


def signed_freq(length):
    indices = jnp.arange(length, dtype=jnp.int32)
    return jnp.where(indices < length // 2, indices, indices - length).astype(jnp.float32)


def coulomb(width_x, width_y, width_z):
    freq_x = signed_freq(width_x)
    freq_y = signed_freq(width_y)
    freq_z = signed_freq(width_z)
    square = freq_x[:, None, None] * freq_x[:, None, None] + freq_y[None, :, None] * freq_y[None, :, None] + freq_z[None, None, :] * freq_z[None, None, :]
    return jnp.where(square > 0, coulomb_scale / jnp.maximum(square, 1.0), 0.0)


def reference(orbitals):
    block_count = ORBITALS // ORB_DEV
    blocks = orbitals.reshape((block_count, ORB_DEV, NX, NY, NZ))
    kernel = coulomb(NX, NY, NZ)

    def potential(density):
        return jnp.real(jnp.fft.ifftn(kernel * jnp.fft.fftn(density))).astype(blocks.dtype)

    summed = jnp.zeros_like(blocks)
    for distance in (1, 2):
        partner = jnp.roll(blocks, distance, axis=0)

        def one_block(pair_blocks):
            own_block, other_block = pair_blocks
            density = own_block[:, None] * other_block[None, :]
            flattened = density.reshape((ORB_DEV * ORB_DEV, NX, NY, NZ))
            pair_potential = lax.map(potential, flattened).reshape((ORB_DEV, ORB_DEV, NX, NY, NZ))
            home_term = jnp.sum(pair_potential * other_block[None], axis=1)
            carried = jnp.sum(pair_potential * own_block[:, None], axis=0)
            return home_term, carried

        home_term, carried = lax.map(one_block, (blocks, partner))
        summed = summed - home_term - jnp.roll(carried, -distance, axis=0)
    return summed.reshape(orbitals.shape)
```

```python
import functools
import math

import jax
import jax.numpy as jnp
import numpy as np
from jax import lax
from jax.experimental import pallas as pl
from jax.experimental.pallas import tpu as pltpu
from jax.sharding import PartitionSpec as P

coulomb_scale = 64.0
MESH = pl.DeviceIdType.MESH


def tables(length):
    indices = np.arange(length)
    angles = (indices[:, None] * indices[None, :] % length) * (2.0 * math.pi / length)
    cosine, sine = np.cos(angles), np.sin(angles)
    matrix = np.block([[cosine, -sine], [sine, cosine]]).astype(np.float32)
    lead = matrix.astype(jnp.bfloat16)
    rest = (matrix - lead.astype(np.float32)).astype(jnp.bfloat16)
    return lead, rest, lead.T.copy(), rest.T.copy()


def parts(value):
    lead = value.astype(jnp.bfloat16)
    return lead, (value - lead.astype(jnp.float32)).astype(jnp.bfloat16)


def dot(left, right):
    return jnp.dot(left, right, preferred_element_type=jnp.float32)


def times_table(value, lead, rest):
    value_lead, value_rest = parts(value)
    return dot(value_lead, lead) + (dot(value_rest, lead) + dot(value_lead, rest))


def table_times(lead, rest, value):
    value_lead, value_rest = parts(value)
    return dot(lead, value_lead) + (dot(lead, value_rest) + dot(rest, value_lead))


def kernel(
    bands, peers, planes,
    orb, m_lead, m_rest, t_lead, t_rest, out,
    near, far, send, recv, back, home, far_sum, far_got, near_sum, near_got,
    near_s, near_r, far_s, far_r, fwd_s, fwd_r, bwd_s, bwd_r, cfar_s, cfar_r, cnear_s, cnear_r,
):
    local_x, width_y, width_z = orb.shape
    width_x = local_x * peers
    local_y = width_y // peers
    chunks = local_x // planes
    rows = planes * local_y
    me = lax.axis_index("grid")
    block = lax.axis_index("band")
    ahead = lax.rem(block + 1, bands)
    behind = lax.rem(block + bands - 1, bands)

    def to_band(src, dst, chunk, send_sem, recv_sem, target):
        span = pl.ds(chunk * planes, planes)
        return pltpu.make_async_remote_copy(
            src_ref=src.at[span], dst_ref=dst.at[span],
            send_sem=send_sem.at[chunk], recv_sem=recv_sem.at[chunk],
            device_id=(target, me), device_id_type=MESH,
        )

    def near_copy(c):
        return to_band(orb, near, c, near_s, near_r, ahead)

    def far_copy(c):
        return to_band(near, far, c, far_s, far_r, ahead)

    def far_carry(c):
        return to_band(far_sum, far_got, c, cfar_s, cfar_r, behind)

    def near_carry(c):
        return to_band(near_sum, near_got, c, cnear_s, cnear_r, behind)

    def forward(c, d):
        target = lax.rem(me + d, peers)
        return pltpu.make_async_remote_copy(
            src_ref=send.at[:, target, pl.ds(c * rows, rows), :],
            dst_ref=recv.at[:, pl.ds((me * local_x + c * planes) * local_y, rows), :],
            send_sem=fwd_s.at[c, d - 1], recv_sem=fwd_r.at[c, d - 1],
            device_id=(block, target), device_id_type=MESH,
        )

    def backward(c, d):
        target = lax.rem(me + d, peers)
        return pltpu.make_async_remote_copy(
            src_ref=back.at[:, pl.ds((target * local_x + c * planes) * local_y, rows), :],
            dst_ref=home.at[:, me, pl.ds(c * rows, rows), :],
            send_sem=bwd_s.at[c, d - 1], recv_sem=bwd_r.at[c, d - 1],
            device_id=(block, target), device_id_type=MESH,
        )

    barrier = pltpu.get_barrier_semaphore()
    pl.semaphore_signal(barrier, inc=1, device_id=(ahead, me), device_id_type=MESH)
    pl.semaphore_signal(barrier, inc=1, device_id=(behind, me), device_id_type=MESH)
    for d in range(1, peers):
        pl.semaphore_signal(
            barrier, inc=1, device_id=(block, lax.rem(me + d, peers)), device_id_type=MESH
        )
    pl.semaphore_wait(barrier, peers + 1)

    lead_start = min(2, chunks)
    for c in range(lead_start):
        near_copy(c).start()

    def transform_chunk(c):
        span = pl.ds(c * planes, planes)
        own = orb[span]
        real = (own * near[span]).reshape(planes * width_y, width_z)
        imag = (own * far[span]).reshape(planes * width_y, width_z)
        both = times_table(
            jnp.concatenate([real, imag], axis=1), m_lead[...], m_rest[...]
        )
        stacked = jnp.concatenate(
            [
                jnp.concatenate(
                    [
                        both[p * width_y : (p + 1) * width_y, :width_z],
                        both[p * width_y : (p + 1) * width_y, width_z:],
                    ],
                    axis=0,
                )
                for p in range(planes)
            ],
            axis=1,
        )
        result = table_times(t_lead[...], t_rest[...], stacked)
        for p in range(planes):
            for part in range(2):
                for g in range(peers):
                    at = part * width_y + g * local_y
                    send[part, g, pl.ds(c * rows + p * local_y, local_y), :] = result[
                        at : at + local_y, p * width_z : (p + 1) * width_z
                    ]
        for part in range(2):
            recv[part, pl.ds((me * local_x + c * planes) * local_y, rows), :] = send[
                part, me, pl.ds(c * rows, rows), :
            ]

    def inbound(s, carry):
        @pl.when(s < chunks)
        def _():
            near_copy(s).wait_recv()
            far_copy(s).start()

            @pl.when(s + lead_start < chunks)
            def _():
                near_copy(s + lead_start).start()

        @pl.when(s > 0)
        def _():
            c = s - 1
            far_copy(c).wait_recv()
            transform_chunk(c)
            for d in range(1, peers):
                forward(c, d).start()

        return carry

    lax.fori_loop(0, chunks + 1, inbound, 0)

    def arrived(c, carry):
        for d in range(1, peers):
            forward(c, d).wait_recv()
        return carry

    lax.fori_loop(0, chunks, arrived, 0)

    def signed(index, length):
        return jnp.where(index < length // 2, index, index - length).astype(jnp.float32)

    freq_x = signed(lax.broadcasted_iota(jnp.int32, (width_x, width_z), 0), width_x)
    freq_z = signed(lax.broadcasted_iota(jnp.int32, (width_x, width_z), 1), width_z)
    square_xz = freq_x * freq_x + freq_z * freq_z
    scale = coulomb_scale / float(width_x * width_y * width_z)
    group = 2

    def columns(s, carry):
        loaded = []
        weights = []
        for u in range(group):
            j = s * group + u
            line = pl.ds(j, width_x, stride=local_y)
            loaded.append(jnp.concatenate([recv[0, line, :], recv[1, line, :]], axis=0))
            freq_y = signed(me * local_y + j, width_y)
            square = square_xz + freq_y * freq_y
            weight = jnp.where(square > 0, scale / jnp.maximum(square, 1.0), 0.0)
            weights.append(jnp.concatenate([weight, weight], axis=0))
        field = table_times(t_lead[...], t_rest[...], jnp.concatenate(loaded, axis=1))
        field = field * jnp.concatenate(weights, axis=1)
        field = table_times(m_lead[...], m_rest[...], field)
        for u in range(group):
            line = pl.ds(s * group + u, width_x, stride=local_y)
            for part in range(2):
                back[part, line, :] = field[
                    part * width_x : (part + 1) * width_x, u * width_z : (u + 1) * width_z
                ]
        return carry

    lax.fori_loop(0, local_y // group, columns, 0)

    def send_back(c, carry):
        for d in range(1, peers):
            backward(c, d).start()
        for part in range(2):
            home[part, me, pl.ds(c * rows, rows), :] = back[
                part, pl.ds((me * local_x + c * planes) * local_y, rows), :
            ]
        return carry

    lax.fori_loop(0, chunks, send_back, 0)

    def apply_chunk(c):
        span = pl.ds(c * planes, planes)
        stacked = jnp.concatenate(
            [
                jnp.concatenate(
                    [
                        home[part, g, pl.ds(c * rows + p * local_y, local_y), :]
                        for part in range(2)
                        for g in range(peers)
                    ],
                    axis=0,
                )
                for p in range(planes)
            ],
            axis=1,
        )
        both = table_times(m_lead[...], m_rest[...], stacked)
        joined = jnp.concatenate(
            [
                jnp.concatenate(
                    [
                        both[:width_y, p * width_z : (p + 1) * width_z],
                        both[width_y:, p * width_z : (p + 1) * width_z],
                    ],
                    axis=1,
                )
                for p in range(planes)
            ],
            axis=0,
        )
        both = times_table(joined, t_lead[...], t_rest[...])
        near_pot = both[:, :width_z].reshape(planes, width_y, width_z)
        far_pot = both[:, width_z:].reshape(planes, width_y, width_z)
        own = orb[span]
        far_sum[span] = far_pot * own
        near_sum[span] = near_pot * own
        out[span] = -(near_pot * near[span] + far_pot * far[span])

    def outbound(s, carry):
        @pl.when(s < chunks)
        def _():
            for d in range(1, peers):
                backward(s, d).wait_recv()
            apply_chunk(s)
            far_carry(s).start()

        @pl.when((s > 0) & (s <= chunks))
        def _():
            c = s - 1
            span = pl.ds(c * planes, planes)
            far_carry(c).wait_recv()
            near_sum[span] = near_sum[span] + far_got[span]
            near_carry(c).start()

        @pl.when(s > 1)
        def _():
            c = s - 2
            span = pl.ds(c * planes, planes)
            near_carry(c).wait_recv()
            out[span] = out[span] - near_got[span]

        return carry

    lax.fori_loop(0, chunks + 2, outbound, 0)

    def drain(c, carry):
        near_copy(c).wait_send()
        far_copy(c).wait_send()
        far_carry(c).wait_send()
        near_carry(c).wait_send()
        for d in range(1, peers):
            forward(c, d).wait_send()
            backward(c, d).wait_send()
        return carry

    lax.fori_loop(0, chunks, drain, 0)


def per_device(bands, peers, orbitals):
    _, local_x, width_y, width_z = orbitals.shape
    width_x = local_x * peers
    local_y = width_y // peers
    planes = math.gcd(4, local_x)
    chunks = local_x // planes
    slab = pltpu.VMEM((local_x, width_y, width_z), jnp.float32)
    by_peer = pltpu.VMEM((2, peers, local_x * local_y, width_z), jnp.float32)
    by_line = pltpu.VMEM((2, width_x * local_y, width_z), jnp.float32)
    dma = pltpu.SemaphoreType.DMA
    result = pl.pallas_call(
        functools.partial(kernel, bands, peers, planes),
        out_shape=jax.ShapeDtypeStruct((local_x, width_y, width_z), jnp.float32),
        in_specs=[pl.BlockSpec(memory_space=pltpu.VMEM)] * 5,
        out_specs=pl.BlockSpec(memory_space=pltpu.VMEM),
        scratch_shapes=[slab, slab, by_peer, by_line, by_line, by_peer, slab, slab, slab, slab]
        + [dma((chunks,))] * 4
        + [dma((chunks, peers - 1))] * 4
        + [dma((chunks,))] * 4,
        compiler_params=pltpu.CompilerParams(
            collective_id=0, has_side_effects=True, vmem_limit_bytes=52 * 2**20
        ),
        name="exchange",
    )(orbitals[0], *tables(width_z))
    return result[None]


def solution(mesh):
    spec = P("band", "grid", None, None)
    body = functools.partial(per_device, mesh.shape["band"], mesh.shape["grid"])
    return jax.shard_map(body, mesh=mesh, in_specs=(spec,), out_specs=spec, check_vma=False)
```

```python
import functools
import math

import jax
import jax.numpy as jnp
import numpy as np
from jax import lax
from jax.experimental import pallas as pl
from jax.experimental.pallas import tpu as pltpu
from jax.sharding import PartitionSpec as P

coulomb_scale = 64.0
MESH = pl.DeviceIdType.MESH


def table(length):
    indices = np.arange(length)
    angles = (indices[:, None] * indices[None, :] % length) * (2.0 * math.pi / length)
    matrix = (np.cos(angles) + np.sin(angles)).astype(np.float32)
    lead = matrix.astype(jnp.bfloat16)
    rest = (matrix - lead.astype(np.float32)).astype(jnp.bfloat16)
    return np.block([[lead, rest], [lead, rest], [lead, lead]])


def parts(value):
    lead = value.astype(jnp.bfloat16)
    return lead, (value - lead.astype(jnp.float32)).astype(jnp.bfloat16)


def dot(left, right):
    return jnp.dot(left, right, preferred_element_type=jnp.float32)


def kernel(
    bands, peers, planes,
    orb_hbm, tab_hbm, out,
    orb, tab, weight, near, far, sends, recvs, backs, homes, far_sum, far_got, near_sum, near_got,
    in_s, near_s, near_r, far_s, far_r, cfar_s, cfar_r, cnear_s, cnear_r, fwd_s, fwd_r, bwd_s, bwd_r,
):
    local_x, width_y, width_z = orb.shape
    width_x = local_x * peers
    local_y = width_y // peers
    chunks = local_x // planes
    rows = planes * local_y
    half = chunks // 2
    me = lax.axis_index("grid")
    block = lax.axis_index("band")
    ahead = lax.rem(block + 1, bands)
    behind = lax.rem(block + bands - 1, bands)

    orb_in = pltpu.make_async_copy(orb_hbm, orb, in_s.at[0])
    tab_in = pltpu.make_async_copy(tab_hbm, tab, in_s.at[1])
    orb_in.start()
    tab_in.start()

    def to_band(src, dst, chunk, send_sem, recv_sem, target):
        span = pl.ds(chunk * planes, planes)
        return pltpu.make_async_remote_copy(
            src_ref=src.at[span], dst_ref=dst.at[span],
            send_sem=send_sem.at[chunk], recv_sem=recv_sem.at[chunk],
            device_id=(target, me), device_id_type=MESH,
        )

    def near_copy(c):
        return to_band(orb, near, c, near_s, near_r, ahead)

    def far_copy(c):
        return to_band(near, far, c, far_s, far_r, ahead)

    def far_carry(c):
        return to_band(far_sum, far_got, c, cfar_s, cfar_r, behind)

    def near_carry(c):
        return to_band(near_sum, near_got, c, cnear_s, cnear_r, behind)

    def own_lines(c):
        return pl.ds((me * local_x + c * planes) * local_y, rows)

    def forward(which, c, d):
        target = lax.rem(me + d, peers)
        return pltpu.make_async_remote_copy(
            src_ref=sends.at[which, target, pl.ds(c * rows, rows), :],
            dst_ref=recvs.at[which, own_lines(c), :],
            send_sem=fwd_s.at[which, c, d - 1], recv_sem=fwd_r.at[which, c, d - 1],
            device_id=(block, target), device_id_type=MESH,
        )

    def backward(which, c, d):
        target = lax.rem(me + d, peers)
        return pltpu.make_async_remote_copy(
            src_ref=backs.at[which, pl.ds((target * local_x + c * planes) * local_y, rows), :],
            dst_ref=homes.at[which, me, pl.ds(c * rows, rows), :],
            send_sem=bwd_s.at[which, c, d - 1], recv_sem=bwd_r.at[which, c, d - 1],
            device_id=(block, target), device_id_type=MESH,
        )

    barrier = pltpu.get_barrier_semaphore()
    pl.semaphore_signal(barrier, inc=1, device_id=(ahead, me), device_id_type=MESH)
    pl.semaphore_signal(barrier, inc=1, device_id=(behind, me), device_id_type=MESH)
    for d in range(1, peers):
        pl.semaphore_signal(
            barrier, inc=1, device_id=(block, lax.rem(me + d, peers)), device_id_type=MESH
        )
    pl.semaphore_wait(barrier, peers + 1)
    orb_in.wait()

    near_lead = min(3, chunks)
    far_lead = min(2, chunks)
    for c in range(near_lead):
        near_copy(c).start()
    tab_in.wait()

    def signed(index, length):
        return jnp.where(index < length // 2, index, index - length).astype(jnp.float32)

    freq_x = signed(lax.broadcasted_iota(jnp.int32, (width_x, width_z), 0), width_x)
    freq_z = signed(lax.broadcasted_iota(jnp.int32, (width_x, width_z), 1), width_z)
    square_xz = freq_x * freq_x + freq_z * freq_z
    scale = coulomb_scale / float(width_x * width_y * width_z)

    def weigh(j, carry):
        freq_y = signed(me * local_y + j, width_y)
        square = square_xz + freq_y * freq_y
        weight[j] = jnp.where(square > 0, scale / jnp.maximum(square, 1.0), 0.0)
        return carry

    lax.fori_loop(0, local_y, weigh, 0)

    def along_lanes(value):
        lead, rest = parts(value)
        return dot(jnp.concatenate([lead, rest], axis=1), tab[: 2 * width_z, :width_z]) + dot(
            lead, tab[:width_z, width_z:]
        )

    def along_rows(value):
        lead, rest = parts(value)
        length = value.shape[0]
        return dot(tab[2 * length :, :], jnp.concatenate([lead, rest], axis=0)) + dot(
            tab[:length, length:], lead
        )

    def transform_chunk(which, partner, c):
        span = pl.ds(c * planes, planes)
        density = (orb[span] * partner[span]).reshape(planes * width_y, width_z)
        density = along_lanes(density)
        result = along_rows(
            jnp.concatenate(
                [density[p * width_y : (p + 1) * width_y] for p in range(planes)], axis=1
            )
        )
        for p in range(planes):
            for g in range(peers):
                sends[which, g, pl.ds(c * rows + p * local_y, local_y), :] = result[
                    g * local_y : (g + 1) * local_y, p * width_z : (p + 1) * width_z
                ]
        for d in range(1, peers):
            forward(which, c, d).start()
        recvs[which, own_lines(c), :] = sends[which, me, pl.ds(c * rows, rows), :]

    def all_arrived(which):
        def arrived(c, carry):
            for d in range(1, peers):
                forward(which, c, d).wait_recv()
            return carry

        lax.fori_loop(0, chunks, arrived, 0)

    group = math.gcd(4, local_y)
    groups = local_y // group
    per_step = -(-groups // (chunks - half))

    def columns(which, s):
        lines = [pl.ds(s * group + u, width_x, stride=local_y) for u in range(group)]
        field = jnp.concatenate([recvs[which, line, :] for line in lines], axis=1)
        field = along_rows(field) * jnp.concatenate(
            [weight[s * group + u] for u in range(group)], axis=1
        )
        field = along_rows(field)
        for u in range(group):
            backs[which, lines[u], :] = field[:, u * width_z : (u + 1) * width_z]

    def send_back(which, c):
        for d in range(1, peers):
            backward(which, c, d).start()
        homes[which, me, pl.ds(c * rows, rows), :] = backs[which, own_lines(c), :]

    def potential(which, c):
        for d in range(1, peers):
            backward(which, c, d).wait_recv()
        stacked = jnp.concatenate(
            [
                jnp.concatenate(
                    [
                        homes[which, g, pl.ds(c * rows + p * local_y, local_y), :]
                        for g in range(peers)
                    ],
                    axis=0,
                )
                for p in range(planes)
            ],
            axis=1,
        )
        turned = along_rows(stacked)
        joined = jnp.concatenate(
            [turned[:, p * width_z : (p + 1) * width_z] for p in range(planes)], axis=0
        )
        return along_lanes(joined).reshape(planes, width_y, width_z)

    def apply_near(c):
        span = pl.ds(c * planes, planes)
        pot = potential(0, c)
        near_sum[span] = pot * orb[span]
        out[span] = -(pot * near[span])

    def apply_far(c):
        span = pl.ds(c * planes, planes)
        pot = potential(1, c)
        far_sum[span] = pot * orb[span]
        far_carry(c).start()
        out[span] = out[span] - pot * far[span]

    def near_in(c, carry):
        near_copy(c).wait_recv()

        @pl.when(c + near_lead < chunks)
        def _():
            near_copy(c + near_lead).start()

        @pl.when(c >= chunks - far_lead)
        def _():
            far_copy(c - (chunks - far_lead)).start()

        transform_chunk(0, near, c)
        return carry

    lax.fori_loop(0, chunks, near_in, 0)

    def far_in(c, carry):
        far_copy(c).wait_recv()

        @pl.when(c + far_lead < chunks)
        def _():
            far_copy(c + far_lead).start()

        transform_chunk(1, far, c)

        @pl.when(c == half)
        def _():
            all_arrived(0)

        @pl.when(c >= half)
        def _():
            for u in range(per_step):
                s = (c - half) * per_step + u

                @pl.when(s < groups)
                def _():
                    columns(0, s)

        return carry

    lax.fori_loop(0, chunks, far_in, 0)

    def back_first(c, carry):
        send_back(0, c)
        return carry

    lax.fori_loop(0, half, back_first, 0)
    all_arrived(1)

    def far_columns(s, carry):
        columns(1, s)
        return carry

    lax.fori_loop(0, groups, far_columns, 0)

    def back_both(c, carry):
        send_back(1, c)

        @pl.when(c + half < chunks)
        def _():
            send_back(0, c + half)

        return carry

    lax.fori_loop(0, chunks, back_both, 0)

    def apply_first(c, carry):
        apply_near(c)
        return carry

    lax.fori_loop(0, half, apply_first, 0)

    def outbound(s, carry):
        @pl.when(s < chunks)
        def _():
            apply_far(s)

        @pl.when(s + half < chunks)
        def _():
            apply_near(s + half)

        @pl.when((s > 0) & (s <= chunks))
        def _():
            c = s - 1
            span = pl.ds(c * planes, planes)
            far_carry(c).wait_recv()
            near_sum[span] = near_sum[span] + far_got[span]
            near_carry(c).start()

        @pl.when(s > 1)
        def _():
            c = s - 2
            span = pl.ds(c * planes, planes)
            near_carry(c).wait_recv()
            out[span] = out[span] - near_got[span]

        return carry

    lax.fori_loop(0, chunks + 2, outbound, 0)

    def drain(c, carry):
        near_copy(c).wait_send()
        far_copy(c).wait_send()
        far_carry(c).wait_send()
        near_carry(c).wait_send()
        for which in range(2):
            for d in range(1, peers):
                forward(which, c, d).wait_send()
                backward(which, c, d).wait_send()
        return carry

    lax.fori_loop(0, chunks, drain, 0)


def per_device(bands, peers, orbitals):
    _, local_x, width_y, width_z = orbitals.shape
    width_x = local_x * peers
    local_y = width_y // peers
    planes = math.gcd(4, local_x)
    chunks = local_x // planes
    slab = pltpu.VMEM((local_x, width_y, width_z), jnp.float32)
    by_peer = pltpu.VMEM((2, peers, local_x * local_y, width_z), jnp.float32)
    by_line = pltpu.VMEM((2, width_x * local_y, width_z), jnp.float32)
    dma = pltpu.SemaphoreType.DMA
    result = pl.pallas_call(
        functools.partial(kernel, bands, peers, planes),
        out_shape=jax.ShapeDtypeStruct((local_x, width_y, width_z), jnp.float32),
        in_specs=[pl.BlockSpec(memory_space=pl.ANY)] * 2,
        out_specs=pl.BlockSpec(memory_space=pltpu.VMEM),
        scratch_shapes=[slab, pltpu.VMEM((3 * width_z, 2 * width_z), jnp.bfloat16)]
        + [pltpu.VMEM((local_y, width_x, width_z), jnp.float32)]
        + [slab, slab, by_peer, by_line, by_line, by_peer, slab, slab, slab, slab]
        + [dma((2,))]
        + [dma((chunks,))] * 8
        + [dma((2, chunks, peers - 1))] * 4,
        compiler_params=pltpu.CompilerParams(
            collective_id=0, has_side_effects=True, vmem_limit_bytes=60 * 2**20
        ),
        name="exchange",
    )(orbitals[0], table(width_z))
    return result[None]


def solution(mesh):
    spec = P("band", "grid", None, None)
    body = functools.partial(per_device, mesh.shape["band"], mesh.shape["grid"])
    return jax.shard_map(body, mesh=mesh, in_specs=(spec,), out_specs=spec, check_vma=False)
```

```python
import functools
import math

import jax
import jax.numpy as jnp
import numpy as np
from jax import lax
from jax.experimental import pallas as pl
from jax.experimental.pallas import tpu as pltpu
from jax.sharding import PartitionSpec as P

coulomb_scale = 64.0
MESH = pl.DeviceIdType.MESH


def table(length):
    indices = np.arange(length)
    angles = (indices[:, None] * indices[None, :] % length) * (2.0 * math.pi / length)
    matrix = (np.cos(angles) + np.sin(angles)).astype(np.float32)
    lead = matrix.astype(jnp.bfloat16)
    rest = (matrix - lead.astype(np.float32)).astype(jnp.bfloat16)
    return np.block([[lead, rest], [lead, rest], [lead, lead]])


def parts(value):
    lead = value.astype(jnp.bfloat16)
    return lead, (value - lead.astype(jnp.float32)).astype(jnp.bfloat16)


def dot(left, right):
    return jnp.dot(left, right, preferred_element_type=jnp.float32)


def kernel(
    bands, peers, planes,
    orb_hbm, tab_hbm, out,
    orb, tab, weight, partner, sends, recvs, backs, homes, sums, far_got, near_got,
    in_s, near_s, near_r, far_s, far_r, cfar_s, cfar_r, cnear_s, cnear_r, fwd_s, fwd_r, bwd_s, bwd_r,
):
    local_x, width_y, width_z = orb.shape
    width_x = local_x * peers
    local_y = width_y // peers
    chunks = local_x // planes
    rows = planes * local_y
    half = max(chunks // 2, 1)
    me = lax.axis_index("grid")
    block = lax.axis_index("band")
    ahead = lax.rem(block + 1, bands)
    behind = lax.rem(block + bands - 1, bands)
    odd = lax.rem(block, 2)
    near, far = partner.at[0], partner.at[1]
    near_sum, far_sum = sums.at[0], sums.at[1]

    orb_in = pltpu.make_async_copy(orb_hbm, orb, in_s.at[0])
    tab_in = pltpu.make_async_copy(tab_hbm, tab, in_s.at[1])
    orb_in.start()
    tab_in.start()

    def to_band(src, dst, chunk, send_sem, recv_sem, target):
        span = pl.ds(chunk * planes, planes)
        return pltpu.make_async_remote_copy(
            src_ref=src.at[span], dst_ref=dst.at[span],
            send_sem=send_sem.at[chunk], recv_sem=recv_sem.at[chunk],
            device_id=(target, me), device_id_type=MESH,
        )

    def near_copy(c):
        return to_band(orb, near, c, near_s, near_r, ahead)

    def far_copy(c):
        return to_band(near, far, c, far_s, far_r, ahead)

    def far_carry(c):
        return to_band(far_sum, far_got, c, cfar_s, cfar_r, behind)

    def near_carry(c):
        return to_band(near_sum, near_got, c, cnear_s, cnear_r, behind)

    def own_lines(c):
        return pl.ds((me * local_x + c * planes) * local_y, rows)

    def forward(which, c, d):
        target = lax.rem(me + d, peers)
        return pltpu.make_async_remote_copy(
            src_ref=sends.at[which, target, pl.ds(c * rows, rows), :],
            dst_ref=recvs.at[which, own_lines(c), :],
            send_sem=fwd_s.at[which, c, d - 1], recv_sem=fwd_r.at[which, c, d - 1],
            device_id=(block, target), device_id_type=MESH,
        )

    def backward(which, c, d):
        target = lax.rem(me + d, peers)
        return pltpu.make_async_remote_copy(
            src_ref=backs.at[which, pl.ds((target * local_x + c * planes) * local_y, rows), :],
            dst_ref=homes.at[which, me, pl.ds(c * rows, rows), :],
            send_sem=bwd_s.at[which, c, d - 1], recv_sem=bwd_r.at[which, c, d - 1],
            device_id=(block, target), device_id_type=MESH,
        )

    barrier = pltpu.get_barrier_semaphore()
    pl.semaphore_signal(barrier, inc=1, device_id=(ahead, me), device_id_type=MESH)
    pl.semaphore_signal(barrier, inc=1, device_id=(behind, me), device_id_type=MESH)
    for d in range(1, peers):
        pl.semaphore_signal(
            barrier, inc=1, device_id=(block, lax.rem(me + d, peers)), device_id_type=MESH
        )
    pl.semaphore_wait(barrier, peers + 1)
    orb_in.wait()

    near_lead = min(3, chunks)
    far_lead = min(2, chunks)
    for c in range(near_lead):
        near_copy(c).start()
    tab_in.wait()

    def signed(index, length):
        return jnp.where(index < length // 2, index, index - length).astype(jnp.float32)

    freq_x = signed(lax.broadcasted_iota(jnp.int32, (width_x, width_z), 0), width_x)
    freq_z = signed(lax.broadcasted_iota(jnp.int32, (width_x, width_z), 1), width_z)
    square_xz = freq_x * freq_x + freq_z * freq_z
    scale = coulomb_scale / float(width_x * width_y * width_z)

    def weigh(j, carry):
        freq_y = signed(me * local_y + j, width_y)
        square = square_xz + freq_y * freq_y
        weight[j] = jnp.where(square > 0, scale / jnp.maximum(square, 1.0), 0.0)
        return carry

    lax.fori_loop(0, local_y, weigh, 0)

    def along_lanes(value):
        lead, rest = parts(value)
        return dot(jnp.concatenate([lead, rest], axis=1), tab[: 2 * width_z, :width_z]) + dot(
            lead, tab[:width_z, width_z:]
        )

    def along_rows(value):
        lead, rest = parts(value)
        length = value.shape[0]
        return dot(tab[2 * length :, :], jnp.concatenate([lead, rest], axis=0)) + dot(
            tab[:length, length:], lead
        )

    def transform_chunk(which, c):
        span = pl.ds(c * planes, planes)
        other = partner[lax.rem(odd + which, 2), span]
        density = (orb[span] * other).reshape(planes * width_y, width_z)
        density = along_lanes(density)
        result = along_rows(
            jnp.concatenate(
                [density[p * width_y : (p + 1) * width_y] for p in range(planes)], axis=1
            )
        )
        for p in range(planes):
            for g in range(peers):
                sends[which, g, pl.ds(c * rows + p * local_y, local_y), :] = result[
                    g * local_y : (g + 1) * local_y, p * width_z : (p + 1) * width_z
                ]
        for d in range(1, peers):
            forward(which, c, d).start()
        recvs[which, own_lines(c), :] = sends[which, me, pl.ds(c * rows, rows), :]

    def all_arrived(which):
        def arrived(c, carry):
            for d in range(1, peers):
                forward(which, c, d).wait_recv()
            return carry

        lax.fori_loop(0, chunks, arrived, 0)

    group = math.gcd(4, local_y)
    groups = local_y // group
    per_step = -(-groups // half)

    def columns(which, s):
        lines = [pl.ds(s * group + u, width_x, stride=local_y) for u in range(group)]
        field = jnp.concatenate([recvs[which, line, :] for line in lines], axis=1)
        field = along_rows(field) * jnp.concatenate(
            [weight[s * group + u] for u in range(group)], axis=1
        )
        field = along_rows(field)
        for u in range(group):
            backs[which, lines[u], :] = field[:, u * width_z : (u + 1) * width_z]

    def send_back(which, c):
        for d in range(1, peers):
            backward(which, c, d).start()
        homes[which, me, pl.ds(c * rows, rows), :] = backs[which, own_lines(c), :]

    def potential(which, c):
        for d in range(1, peers):
            backward(which, c, d).wait_recv()
        stacked = jnp.concatenate(
            [
                jnp.concatenate(
                    [
                        homes[which, g, pl.ds(c * rows + p * local_y, local_y), :]
                        for g in range(peers)
                    ],
                    axis=0,
                )
                for p in range(planes)
            ],
            axis=1,
        )
        turned = along_rows(stacked)
        joined = jnp.concatenate(
            [turned[:, p * width_z : (p + 1) * width_z] for p in range(planes)], axis=0
        )
        return along_lanes(joined).reshape(planes, width_y, width_z)

    def apply(which, c):
        role = lax.rem(odd + which, 2)
        span = pl.ds(c * planes, planes)
        pot = potential(which, c)
        sums[role, span] = pot * orb[span]
        term = pot * partner[role, span]
        if which == 0:
            out[span] = -term
        else:
            out[span] = out[span] - term

        @pl.when(role == 1)
        def _():
            far_carry(c).start()

    def hand_on(which, c):
        @pl.when(lax.rem(odd + which, 2) == 0)
        def _():
            span = pl.ds(c * planes, planes)
            far_carry(c).wait_recv()
            near_sum[span] = near_sum[span] + far_got[span]
            near_carry(c).start()

    def first_in(c, carry):
        @pl.when(odd == 0)
        def _():
            near_copy(c).wait_recv()
            far_copy(c).start()

        @pl.when(c + near_lead < chunks)
        def _():
            near_copy(c + near_lead).start()

        @pl.when((odd == 1) & (c >= chunks - far_lead))
        def _():
            near_copy(c - (chunks - far_lead)).wait_recv()
            far_copy(c - (chunks - far_lead)).start()

        @pl.when(odd == 1)
        def _():
            far_copy(c).wait_recv()

        transform_chunk(0, c)
        return carry

    lax.fori_loop(0, chunks, first_in, 0)

    def second_in(c, carry):
        @pl.when((odd == 1) & (c + far_lead < chunks))
        def _():
            near_copy(c + far_lead).wait_recv()
            far_copy(c + far_lead).start()

        @pl.when(odd == 0)
        def _():
            far_copy(c).wait_recv()

        transform_chunk(1, c)

        @pl.when(c == chunks - half)
        def _():
            all_arrived(0)

        @pl.when(c >= chunks - half)
        def _():
            for u in range(per_step):
                s = (c - (chunks - half)) * per_step + u

                @pl.when(s < groups)
                def _():
                    columns(0, s)

        return carry

    lax.fori_loop(0, chunks, second_in, 0)

    def back_all(which):
        def one(c, carry):
            send_back(which, c)
            return carry

        lax.fori_loop(0, chunks, one, 0)

    back_all(0)

    def first_out(s, carry):
        @pl.when(s < chunks)
        def _():
            apply(0, s)

        @pl.when(s > 0)
        def _():
            hand_on(0, s - 1)

        @pl.when(s == 0)
        def _():
            all_arrived(1)

        @pl.when(s < half)
        def _():
            for u in range(per_step):
                t = s * per_step + u

                @pl.when(t < groups)
                def _():
                    columns(1, t)

        @pl.when(s == half - 1)
        def _():
            back_all(1)

        return carry

    lax.fori_loop(0, chunks + 1, first_out, 0)

    def second_out(s, carry):
        @pl.when(s < chunks)
        def _():
            apply(1, s)

        @pl.when((s > 0) & (s <= chunks))
        def _():
            hand_on(1, s - 1)

        @pl.when(s > 1)
        def _():
            c = s - 2
            span = pl.ds(c * planes, planes)
            near_carry(c).wait_recv()
            out[span] = out[span] - near_got[span]

        return carry

    lax.fori_loop(0, chunks + 2, second_out, 0)

    def drain(c, carry):
        near_copy(c).wait_send()
        far_copy(c).wait_send()
        far_carry(c).wait_send()
        near_carry(c).wait_send()
        for which in range(2):
            for d in range(1, peers):
                forward(which, c, d).wait_send()
                backward(which, c, d).wait_send()
        return carry

    lax.fori_loop(0, chunks, drain, 0)


def per_device(bands, peers, orbitals):
    _, local_x, width_y, width_z = orbitals.shape
    width_x = local_x * peers
    local_y = width_y // peers
    planes = math.gcd(4, local_x)
    chunks = local_x // planes
    slab = pltpu.VMEM((local_x, width_y, width_z), jnp.float32)
    slabs = pltpu.VMEM((2, local_x, width_y, width_z), jnp.float32)
    by_peer = pltpu.VMEM((2, peers, local_x * local_y, width_z), jnp.float32)
    by_line = pltpu.VMEM((2, width_x * local_y, width_z), jnp.float32)
    dma = pltpu.SemaphoreType.DMA
    result = pl.pallas_call(
        functools.partial(kernel, bands, peers, planes),
        out_shape=jax.ShapeDtypeStruct((local_x, width_y, width_z), jnp.float32),
        in_specs=[pl.BlockSpec(memory_space=pl.ANY)] * 2,
        out_specs=pl.BlockSpec(memory_space=pltpu.VMEM),
        scratch_shapes=[slab, pltpu.VMEM((3 * width_z, 2 * width_z), jnp.bfloat16)]
        + [pltpu.VMEM((local_y, width_x, width_z), jnp.float32)]
        + [slabs, by_peer, by_line, by_line, by_peer, slabs, slab, slab]
        + [dma((2,))]
        + [dma((chunks,))] * 8
        + [dma((2, chunks, peers - 1))] * 4,
        compiler_params=pltpu.CompilerParams(
            collective_id=0, has_side_effects=True, vmem_limit_bytes=60 * 2**20
        ),
        name="exchange",
    )(orbitals[0], table(width_z))
    return result[None]


def solution(mesh):
    spec = P("band", "grid", None, None)
    body = functools.partial(per_device, mesh.shape["band"], mesh.shape["grid"])
    return jax.shard_map(body, mesh=mesh, in_specs=(spec,), out_specs=spec, check_vma=False)
```

```python
import functools
import math

import jax
import jax.numpy as jnp
import numpy as np
from jax import lax
from jax.experimental import pallas as pl
from jax.experimental.pallas import tpu as pltpu
from jax.sharding import PartitionSpec as P

coulomb_scale = 64.0
MESH = pl.DeviceIdType.MESH


def table(length):
    indices = np.arange(length)
    angles = (indices[:, None] * indices[None, :] % length) * (2.0 * math.pi / length)
    matrix = (np.cos(angles) + np.sin(angles)).astype(np.float32)
    lead = matrix.astype(jnp.bfloat16)
    rest = (matrix - lead.astype(np.float32)).astype(jnp.bfloat16)
    return np.block([[lead, rest], [lead, rest], [lead, lead]])


def parts(value):
    lead = value.astype(jnp.bfloat16)
    return lead, (value - lead.astype(jnp.float32)).astype(jnp.bfloat16)


def dot(left, right):
    return jnp.dot(left, right, preferred_element_type=jnp.float32)


def kernel(
    bands, peers, planes,
    orb_hbm, tab_hbm, out_hbm,
    out, orb, tab, weight, partner, sends, recvs, backs, homes, sums, far_got, near_got,
    in_s, near_s, near_r, far_s, far_r, cfar_s, cfar_r, cnear_s, cnear_r, fwd_s, fwd_r, bwd_s, bwd_r, out_s,
):
    local_x, width_y, width_z = orb.shape
    width_x = local_x * peers
    local_y = width_y // peers
    chunks = local_x // planes
    rows = planes * local_y
    half = max(chunks // 2, 1)
    me = lax.axis_index("grid")
    block = lax.axis_index("band")
    ahead = lax.rem(block + 1, bands)
    behind = lax.rem(block + bands - 1, bands)
    odd = lax.rem(block, 2)
    near, far = partner.at[0], partner.at[1]
    near_sum, far_sum = sums.at[0], sums.at[1]

    orb_in = pltpu.make_async_copy(orb_hbm, orb, in_s.at[0])
    tab_in = pltpu.make_async_copy(tab_hbm, tab, in_s.at[1])
    orb_in.start()
    tab_in.start()

    def to_band(src, dst, chunk, send_sem, recv_sem, target):
        span = pl.ds(chunk * planes, planes)
        return pltpu.make_async_remote_copy(
            src_ref=src.at[span], dst_ref=dst.at[span],
            send_sem=send_sem.at[chunk], recv_sem=recv_sem.at[chunk],
            device_id=(target, me), device_id_type=MESH,
        )

    def near_copy(c):
        return to_band(orb, near, c, near_s, near_r, ahead)

    def far_copy(c):
        return to_band(near, far, c, far_s, far_r, ahead)

    def far_carry(c):
        return to_band(far_sum, far_got, c, cfar_s, cfar_r, behind)

    def near_carry(c):
        return to_band(near_sum, near_got, c, cnear_s, cnear_r, behind)

    def out_copy(c):
        span = pl.ds(c * planes, planes)
        return pltpu.make_async_copy(out.at[span], out_hbm.at[span], out_s.at[c])

    def own_lines(c):
        return pl.ds((me * local_x + c * planes) * local_y, rows)

    def forward(which, c, d):
        target = lax.rem(me + d, peers)
        return pltpu.make_async_remote_copy(
            src_ref=sends.at[which, target, pl.ds(c * rows, rows), :],
            dst_ref=recvs.at[which, own_lines(c), :],
            send_sem=fwd_s.at[which, c, d - 1], recv_sem=fwd_r.at[which, c, d - 1],
            device_id=(block, target), device_id_type=MESH,
        )

    def backward(which, c, d):
        target = lax.rem(me + d, peers)
        return pltpu.make_async_remote_copy(
            src_ref=backs.at[which, pl.ds((target * local_x + c * planes) * local_y, rows), :],
            dst_ref=homes.at[which, me, pl.ds(c * rows, rows), :],
            send_sem=bwd_s.at[which, c, d - 1], recv_sem=bwd_r.at[which, c, d - 1],
            device_id=(block, target), device_id_type=MESH,
        )

    barrier = pltpu.get_barrier_semaphore()
    pl.semaphore_signal(barrier, inc=1, device_id=(ahead, me), device_id_type=MESH)
    pl.semaphore_signal(barrier, inc=1, device_id=(behind, me), device_id_type=MESH)
    for d in range(1, peers):
        pl.semaphore_signal(
            barrier, inc=1, device_id=(block, lax.rem(me + d, peers)), device_id_type=MESH
        )
    pl.semaphore_wait(barrier, peers + 1)
    orb_in.wait()

    near_lead = min(4, chunks)
    far_lead = min(3, chunks)
    for c in range(near_lead):
        near_copy(c).start()
    tab_in.wait()

    def signed(index, length):
        return jnp.where(index < length // 2, index, index - length).astype(jnp.float32)

    freq_x = signed(lax.broadcasted_iota(jnp.int32, (width_x, width_z), 0), width_x)
    freq_z = signed(lax.broadcasted_iota(jnp.int32, (width_x, width_z), 1), width_z)
    square_xz = freq_x * freq_x + freq_z * freq_z
    scale = coulomb_scale / float(width_x * width_y * width_z)

    def weigh(j, carry):
        freq_y = signed(me * local_y + j, width_y)
        square = square_xz + freq_y * freq_y
        weight[j] = jnp.where(square > 0, scale / jnp.maximum(square, 1.0), 0.0)
        return carry

    lax.fori_loop(0, local_y, weigh, 0)

    def along_lanes(value):
        lead, rest = parts(value)
        return dot(jnp.concatenate([lead, rest], axis=1), tab[: 2 * width_z, :width_z]) + dot(
            lead, tab[:width_z, width_z:]
        )

    def along_rows(value):
        lead, rest = parts(value)
        length = value.shape[0]
        return dot(tab[2 * length :, :], jnp.concatenate([lead, rest], axis=0)) + dot(
            tab[:length, length:], lead
        )

    def transform_chunk(which, c):
        span = pl.ds(c * planes, planes)
        other = partner[lax.rem(odd + which, 2), span]
        density = (orb[span] * other).reshape(planes * width_y, width_z)
        density = along_lanes(density)
        result = along_rows(
            jnp.concatenate(
                [density[p * width_y : (p + 1) * width_y] for p in range(planes)], axis=1
            )
        )
        for p in range(planes):
            for g in range(peers):
                sends[which, g, pl.ds(c * rows + p * local_y, local_y), :] = result[
                    g * local_y : (g + 1) * local_y, p * width_z : (p + 1) * width_z
                ]
        for d in range(1, peers):
            forward(which, c, d).start()
        recvs[which, own_lines(c), :] = sends[which, me, pl.ds(c * rows, rows), :]

    def all_arrived(which):
        def arrived(c, carry):
            for d in range(1, peers):
                forward(which, c, d).wait_recv()
            return carry

        lax.fori_loop(0, chunks, arrived, 0)

    group = math.gcd(4, local_y)
    groups = local_y // group
    per_step = -(-groups // half)

    def columns(which, s):
        lines = [pl.ds(s * group + u, width_x, stride=local_y) for u in range(group)]
        field = jnp.concatenate([recvs[which, line, :] for line in lines], axis=1)
        field = along_rows(field) * jnp.concatenate(
            [weight[s * group + u] for u in range(group)], axis=1
        )
        field = along_rows(field)
        for u in range(group):
            backs[which, lines[u], :] = field[:, u * width_z : (u + 1) * width_z]

    def send_back(which, c):
        for d in range(1, peers):
            backward(which, c, d).start()
        homes[which, me, pl.ds(c * rows, rows), :] = backs[which, own_lines(c), :]

    def potential(which, c):
        for d in range(1, peers):
            backward(which, c, d).wait_recv()
        stacked = jnp.concatenate(
            [
                jnp.concatenate(
                    [
                        homes[which, g, pl.ds(c * rows + p * local_y, local_y), :]
                        for g in range(peers)
                    ],
                    axis=0,
                )
                for p in range(planes)
            ],
            axis=1,
        )
        turned = along_rows(stacked)
        joined = jnp.concatenate(
            [turned[:, p * width_z : (p + 1) * width_z] for p in range(planes)], axis=0
        )
        return along_lanes(joined).reshape(planes, width_y, width_z)

    def apply(which, c):
        role = lax.rem(odd + which, 2)
        span = pl.ds(c * planes, planes)
        pot = potential(which, c)
        sums[role, span] = pot * orb[span]
        term = pot * partner[role, span]
        if which == 0:
            out[span] = -term
        else:
            out[span] = out[span] - term

        @pl.when(role == 1)
        def _():
            far_carry(c).start()

    def hand_on(which, c):
        @pl.when(lax.rem(odd + which, 2) == 0)
        def _():
            span = pl.ds(c * planes, planes)
            far_carry(c).wait_recv()
            near_sum[span] = near_sum[span] + far_got[span]
            near_carry(c).start()

    def first_in(c, carry):
        @pl.when(odd == 0)
        def _():
            near_copy(c).wait_recv()
            far_copy(c).start()

        @pl.when(c + near_lead < chunks)
        def _():
            near_copy(c + near_lead).start()

        @pl.when((odd == 1) & (c >= chunks - far_lead))
        def _():
            near_copy(c - (chunks - far_lead)).wait_recv()
            far_copy(c - (chunks - far_lead)).start()

        @pl.when(odd == 1)
        def _():
            far_copy(c).wait_recv()

        transform_chunk(0, c)
        return carry

    lax.fori_loop(0, chunks, first_in, 0)

    def second_in(c, carry):
        @pl.when((odd == 1) & (c + far_lead < chunks))
        def _():
            near_copy(c + far_lead).wait_recv()
            far_copy(c + far_lead).start()

        @pl.when(odd == 0)
        def _():
            far_copy(c).wait_recv()

        transform_chunk(1, c)

        @pl.when(c == chunks - half)
        def _():
            all_arrived(0)

        @pl.when(c >= chunks - half)
        def _():
            for u in range(per_step):
                s = (c - (chunks - half)) * per_step + u

                @pl.when(s < groups)
                def _():
                    columns(0, s)

        return carry

    lax.fori_loop(0, chunks, second_in, 0)

    def back_all(which):
        def one(c, carry):
            send_back(which, c)
            return carry

        lax.fori_loop(0, chunks, one, 0)

    back_all(0)

    def first_out(s, carry):
        @pl.when(s < chunks)
        def _():
            apply(0, s)

        @pl.when(s > 0)
        def _():
            hand_on(0, s - 1)

        @pl.when(s == 0)
        def _():
            all_arrived(1)

        @pl.when(s < half)
        def _():
            for u in range(per_step):
                t = s * per_step + u

                @pl.when(t < groups)
                def _():
                    columns(1, t)

        @pl.when(s == half - 1)
        def _():
            back_all(1)

        return carry

    lax.fori_loop(0, chunks + 1, first_out, 0)

    def second_out(s, carry):
        @pl.when(s < chunks)
        def _():
            apply(1, s)

        @pl.when((s > 0) & (s <= chunks))
        def _():
            hand_on(1, s - 1)

        @pl.when(s > 1)
        def _():
            c = s - 2
            span = pl.ds(c * planes, planes)
            near_carry(c).wait_recv()
            out[span] = out[span] - near_got[span]
            out_copy(c).start()

        return carry

    lax.fori_loop(0, chunks + 2, second_out, 0)

    def drain(c, carry):
        near_copy(c).wait_send()
        far_copy(c).wait_send()
        far_carry(c).wait_send()
        near_carry(c).wait_send()
        out_copy(c).wait()
        for which in range(2):
            for d in range(1, peers):
                forward(which, c, d).wait_send()
                backward(which, c, d).wait_send()
        return carry

    lax.fori_loop(0, chunks, drain, 0)


def per_device(bands, peers, orbitals):
    _, local_x, width_y, width_z = orbitals.shape
    width_x = local_x * peers
    local_y = width_y // peers
    planes = math.gcd(4, local_x)
    chunks = local_x // planes
    slab = pltpu.VMEM((local_x, width_y, width_z), jnp.float32)
    slabs = pltpu.VMEM((2, local_x, width_y, width_z), jnp.float32)
    by_peer = pltpu.VMEM((2, peers, local_x * local_y, width_z), jnp.float32)
    by_line = pltpu.VMEM((2, width_x * local_y, width_z), jnp.float32)
    dma = pltpu.SemaphoreType.DMA
    result = pl.pallas_call(
        functools.partial(kernel, bands, peers, planes),
        out_shape=jax.ShapeDtypeStruct((local_x, width_y, width_z), jnp.float32),
        in_specs=[pl.BlockSpec(memory_space=pl.ANY)] * 2,
        out_specs=pl.BlockSpec(memory_space=pl.ANY),
        scratch_shapes=[slab, slab, pltpu.VMEM((3 * width_z, 2 * width_z), jnp.bfloat16)]
        + [pltpu.VMEM((local_y, width_x, width_z), jnp.float32)]
        + [slabs, by_peer, by_line, by_line, by_peer, slabs, slab, slab]
        + [dma((2,))]
        + [dma((chunks,))] * 8
        + [dma((2, chunks, peers - 1))] * 4
        + [dma((chunks,))],
        compiler_params=pltpu.CompilerParams(
            collective_id=0, has_side_effects=True, vmem_limit_bytes=60 * 2**20
        ),
        name="exchange",
    )(orbitals[0], table(width_z))
    return result[None]


def solution(mesh):
    spec = P("band", "grid", None, None)
    body = functools.partial(per_device, mesh.shape["band"], mesh.shape["grid"])
    return jax.shard_map(body, mesh=mesh, in_specs=(spec,), out_specs=spec, check_vma=False)
```

```python
import functools
import math

import jax
import jax.numpy as jnp
import numpy as np
from jax import lax
from jax.experimental import pallas as pl
from jax.experimental.pallas import tpu as pltpu
from jax.sharding import PartitionSpec as P

coulomb_scale = 64.0
MESH = pl.DeviceIdType.MESH


def table(length):
    indices = np.arange(length)
    angles = (indices[:, None] * indices[None, :] % length) * (2.0 * math.pi / length)
    matrix = (np.cos(angles) + np.sin(angles)).astype(np.float32)
    lead = matrix.astype(jnp.bfloat16)
    rest = (matrix - lead.astype(np.float32)).astype(jnp.bfloat16)
    return np.block([[lead, rest], [lead, rest], [lead, lead]])


def parts(value):
    lead = value.astype(jnp.bfloat16)
    return lead, (value - lead.astype(jnp.float32)).astype(jnp.bfloat16)


def dot(left, right):
    return jnp.dot(left, right, preferred_element_type=jnp.float32)


def kernel(
    bands, peers, planes,
    orb_hbm, tab_hbm, out_hbm,
    out, orb, tab, weight, partner, sends, recvs, backs, homes, sums, far_got, near_got,
    in_s, near_s, near_r, far_s, far_r, cfar_s, cfar_r, cnear_s, cnear_r, fwd_s, fwd_r, bwd_s, bwd_r, out_s,
):
    local_x, width_y, width_z = orb.shape
    width_x = local_x * peers
    local_y = width_y // peers
    chunks = local_x // planes
    rows = planes * local_y
    half = max(chunks // 2, 1)
    me = lax.axis_index("grid")
    block = lax.axis_index("band")
    ahead = lax.rem(block + 1, bands)
    behind = lax.rem(block + bands - 1, bands)
    odd = lax.rem(block, 2)
    near, far = partner.at[0], partner.at[1]
    near_sum, far_sum = sums.at[0], sums.at[1]

    orb_in = pltpu.make_async_copy(orb_hbm, orb, in_s.at[0])
    tab_in = pltpu.make_async_copy(tab_hbm, tab, in_s.at[1])
    orb_in.start()
    tab_in.start()

    def to_band(src, dst, chunk, send_sem, recv_sem, target):
        span = pl.ds(chunk * planes, planes)
        return pltpu.make_async_remote_copy(
            src_ref=src.at[span], dst_ref=dst.at[span],
            send_sem=send_sem.at[chunk], recv_sem=recv_sem.at[chunk],
            device_id=(target, me), device_id_type=MESH,
        )

    def near_copy(c):
        return to_band(orb, near, c, near_s, near_r, ahead)

    def far_copy(c):
        return to_band(near, far, c, far_s, far_r, ahead)

    def far_carry(c):
        return to_band(far_sum, far_got, c, cfar_s, cfar_r, behind)

    def near_carry(c):
        return to_band(near_sum, near_got, c, cnear_s, cnear_r, behind)

    def out_copy(c):
        span = pl.ds(c * planes, planes)
        return pltpu.make_async_copy(out.at[span], out_hbm.at[span], out_s.at[c])

    def own_lines(c):
        return pl.ds((me * local_x + c * planes) * local_y, rows)

    def forward(which, c, d):
        target = lax.rem(me + d, peers)
        return pltpu.make_async_remote_copy(
            src_ref=sends.at[which, target, pl.ds(c * rows, rows), :],
            dst_ref=recvs.at[which, own_lines(c), :],
            send_sem=fwd_s.at[which, c, d - 1], recv_sem=fwd_r.at[which, c, d - 1],
            device_id=(block, target), device_id_type=MESH,
        )

    def backward(which, c, d):
        target = lax.rem(me + d, peers)
        return pltpu.make_async_remote_copy(
            src_ref=backs.at[which, pl.ds((target * local_x + c * planes) * local_y, rows), :],
            dst_ref=homes.at[which, me, pl.ds(c * rows, rows), :],
            send_sem=bwd_s.at[which, c, d - 1], recv_sem=bwd_r.at[which, c, d - 1],
            device_id=(block, target), device_id_type=MESH,
        )

    barrier = pltpu.get_barrier_semaphore()
    pl.semaphore_signal(barrier, inc=1, device_id=(ahead, me), device_id_type=MESH)
    pl.semaphore_signal(barrier, inc=1, device_id=(behind, me), device_id_type=MESH)
    for d in range(1, peers):
        pl.semaphore_signal(
            barrier, inc=1, device_id=(block, lax.rem(me + d, peers)), device_id_type=MESH
        )
    pl.semaphore_wait(barrier, peers + 1)
    orb_in.wait()

    near_lead = min(4, chunks)
    far_lead = min(3, chunks)
    for c in range(near_lead):
        near_copy(c).start()
    tab_in.wait()

    def signed(index, length):
        return jnp.where(index < length // 2, index, index - length).astype(jnp.float32)

    freq_x = signed(lax.broadcasted_iota(jnp.int32, (width_x, width_z), 0), width_x)
    freq_z = signed(lax.broadcasted_iota(jnp.int32, (width_x, width_z), 1), width_z)
    square_xz = freq_x * freq_x + freq_z * freq_z
    scale = coulomb_scale / float(width_x * width_y * width_z)

    def weigh(j, carry):
        freq_y = signed(me * local_y + j, width_y)
        square = square_xz + freq_y * freq_y
        weight[j] = jnp.where(square > 0, scale / jnp.maximum(square, 1.0), 0.0)
        return carry

    lax.fori_loop(0, local_y, weigh, 0)

    def along_lanes(value):
        lead, rest = parts(value)
        return dot(jnp.concatenate([lead, rest], axis=1), tab[: 2 * width_z, :width_z]) + dot(
            lead, tab[:width_z, width_z:]
        )

    def along_rows(value):
        lead, rest = parts(value)
        length = value.shape[0]
        return dot(tab[2 * length :, :], jnp.concatenate([lead, rest], axis=0)) + dot(
            tab[:length, length:], lead
        )

    def transform_chunk(which, c):
        span = pl.ds(c * planes, planes)
        other = partner[lax.rem(odd + which, 2), span]
        density = (orb[span] * other).reshape(planes * width_y, width_z)
        density = along_lanes(density)
        result = along_rows(
            jnp.concatenate(
                [density[p * width_y : (p + 1) * width_y] for p in range(planes)], axis=1
            )
        )
        for p in range(planes):
            for g in range(peers):
                sends[which, g, pl.ds(c * rows + p * local_y, local_y), :] = result[
                    g * local_y : (g + 1) * local_y, p * width_z : (p + 1) * width_z
                ]
        for d in range(1, peers):
            forward(which, c, d).start()
        recvs[which, own_lines(c), :] = sends[which, me, pl.ds(c * rows, rows), :]

    def all_arrived(which):
        def arrived(c, carry):
            for d in range(1, peers):
                forward(which, c, d).wait_recv()
            return carry

        lax.fori_loop(0, chunks, arrived, 0)

    group = math.gcd(4, local_y)
    groups = local_y // group
    per_step = -(-groups // half)

    def columns(which, s):
        lines = [pl.ds(s * group + u, width_x, stride=local_y) for u in range(group)]
        field = jnp.concatenate([recvs[which, line, :] for line in lines], axis=1)
        field = along_rows(field) * jnp.concatenate(
            [weight[s * group + u] for u in range(group)], axis=1
        )
        field = along_rows(field)
        for u in range(group):
            backs[which, lines[u], :] = field[:, u * width_z : (u + 1) * width_z]

    def send_back(which, c):
        for d in range(1, peers):
            backward(which, c, d).start()
        homes[which, me, pl.ds(c * rows, rows), :] = backs[which, own_lines(c), :]

    def potential(which, c):
        for d in range(1, peers):
            backward(which, c, d).wait_recv()
        stacked = jnp.concatenate(
            [
                jnp.concatenate(
                    [
                        homes[which, g, pl.ds(c * rows + p * local_y, local_y), :]
                        for g in range(peers)
                    ],
                    axis=0,
                )
                for p in range(planes)
            ],
            axis=1,
        )
        turned = along_rows(stacked)
        joined = jnp.concatenate(
            [turned[:, p * width_z : (p + 1) * width_z] for p in range(planes)], axis=0
        )
        return along_lanes(joined).reshape(planes, width_y, width_z)

    def apply(which, c):
        role = lax.rem(odd + which, 2)
        span = pl.ds(c * planes, planes)
        pot = potential(which, c)
        sums[role, span] = pot * orb[span]
        term = pot * partner[role, span]
        if which == 0:
            out[span] = -term
        else:
            out[span] = out[span] - term

        @pl.when(role == 1)
        def _():
            far_carry(c).start()

    def hand_on(which, c):
        @pl.when(lax.rem(odd + which, 2) == 0)
        def _():
            span = pl.ds(c * planes, planes)
            far_carry(c).wait_recv()
            near_sum[span] = near_sum[span] + far_got[span]
            near_carry(c).start()

    def first_in(c, carry):
        @pl.when(odd == 0)
        def _():
            near_copy(c).wait_recv()
            far_copy(c).start()

        @pl.when(c + near_lead < chunks)
        def _():
            near_copy(c + near_lead).start()

        @pl.when((odd == 1) & (c >= chunks - far_lead))
        def _():
            near_copy(c - (chunks - far_lead)).wait_recv()
            far_copy(c - (chunks - far_lead)).start()

        @pl.when(odd == 1)
        def _():
            far_copy(c).wait_recv()

        transform_chunk(0, c)
        return carry

    lax.fori_loop(0, chunks, first_in, 0)

    def second_in(c, carry):
        @pl.when((odd == 1) & (c + far_lead < chunks))
        def _():
            near_copy(c + far_lead).wait_recv()
            far_copy(c + far_lead).start()

        @pl.when(odd == 0)
        def _():
            far_copy(c).wait_recv()

        transform_chunk(1, c)

        @pl.when(c == chunks - half)
        def _():
            all_arrived(0)

        @pl.when(c >= chunks - half)
        def _():
            for u in range(per_step):
                s = (c - (chunks - half)) * per_step + u

                @pl.when(s < groups)
                def _():
                    columns(0, s)

        return carry

    lax.fori_loop(0, chunks, second_in, 0)

    def back_all(which):
        def one(c, carry):
            send_back(which, c)
            return carry

        lax.fori_loop(0, chunks, one, 0)

    back_all(0)

    def first_out(s, carry):
        @pl.when(s < chunks)
        def _():
            apply(0, s)

        @pl.when(s > 0)
        def _():
            hand_on(0, s - 1)

        @pl.when(s == 1)
        def _():
            all_arrived(1)

        @pl.when((s > 0) & (s <= half))
        def _():
            for u in range(per_step):
                t = (s - 1) * per_step + u

                @pl.when(t < groups)
                def _():
                    columns(1, t)

        @pl.when(s == half)
        def _():
            back_all(1)

        return carry

    lax.fori_loop(0, chunks + 1, first_out, 0)

    def second_out(s, carry):
        @pl.when(s < chunks)
        def _():
            apply(1, s)

        @pl.when((s > 0) & (s <= chunks))
        def _():
            hand_on(1, s - 1)

        @pl.when(s > 1)
        def _():
            c = s - 2
            span = pl.ds(c * planes, planes)
            near_carry(c).wait_recv()
            out[span] = out[span] - near_got[span]
            out_copy(c).start()

        return carry

    lax.fori_loop(0, chunks + 2, second_out, 0)

    def drain(c, carry):
        near_copy(c).wait_send()
        far_copy(c).wait_send()
        far_carry(c).wait_send()
        near_carry(c).wait_send()
        out_copy(c).wait()
        for which in range(2):
            for d in range(1, peers):
                forward(which, c, d).wait_send()
                backward(which, c, d).wait_send()
        return carry

    lax.fori_loop(0, chunks, drain, 0)


def per_device(bands, peers, orbitals):
    _, local_x, width_y, width_z = orbitals.shape
    width_x = local_x * peers
    local_y = width_y // peers
    planes = math.gcd(4, local_x)
    chunks = local_x // planes
    slab = pltpu.VMEM((local_x, width_y, width_z), jnp.float32)
    slabs = pltpu.VMEM((2, local_x, width_y, width_z), jnp.float32)
    by_peer = pltpu.VMEM((2, peers, local_x * local_y, width_z), jnp.float32)
    by_line = pltpu.VMEM((2, width_x * local_y, width_z), jnp.float32)
    dma = pltpu.SemaphoreType.DMA
    result = pl.pallas_call(
        functools.partial(kernel, bands, peers, planes),
        out_shape=jax.ShapeDtypeStruct((local_x, width_y, width_z), jnp.float32),
        in_specs=[pl.BlockSpec(memory_space=pl.ANY)] * 2,
        out_specs=pl.BlockSpec(memory_space=pl.ANY),
        scratch_shapes=[slab, slab, pltpu.VMEM((3 * width_z, 2 * width_z), jnp.bfloat16)]
        + [pltpu.VMEM((local_y, width_x, width_z), jnp.float32)]
        + [slabs, by_peer, by_line, by_line, by_peer, slabs, slab, slab]
        + [dma((2,))]
        + [dma((chunks,))] * 8
        + [dma((2, chunks, peers - 1))] * 4
        + [dma((chunks,))],
        compiler_params=pltpu.CompilerParams(
            collective_id=0, has_side_effects=True, vmem_limit_bytes=60 * 2**20
        ),
        name="exchange",
    )(orbitals[0], table(width_z))
    return result[None]


def solution(mesh):
    spec = P("band", "grid", None, None)
    body = functools.partial(per_device, mesh.shape["band"], mesh.shape["grid"])
    return jax.shard_map(body, mesh=mesh, in_specs=(spec,), out_specs=spec, check_vma=False)
```
